128 devices in a mesh: col: 4 (over y_hi, core), row: 32 (over z, y_lo, x).
Axes of the slice: x: 4, y: 4 (y_hi: 2, y_lo: 2; y = y_hi * 2 + y_lo), z: 4, core: 2. Of those that a mesh axis runs over, the one named last changes fastest.
Arguments:
- panel: bfloat16 [32, 48, 512, 128], P('row', 'col'), may hold values from -6 to 6
- stiffness: bfloat16 [32, 48, 512, 512], P('row', 'col'), may hold values from -0.25 to 0.25
- mass: float32 [32, 48, 512], P('row', 'col'), may hold values from 0.2 to 2
- resident: bfloat16 [32, 24576, 1024], P('row', None, 'col'), may hold values from -0.013671875 to 0.013671875
- face_rows: int32 [32, 2, 2048], P('row'), may hold values from 0 to 24575, as said below
- counts: int32 [32], P('row'), may hold values from 24 to 48, as said below
Outputs:
- gram: float32 [1024, 128], P(('col', 'row'))
The draws below stay inside these ranges and needn't reach their ends.
Inputs may be any that keep to these rules, and one draw needn't show every extreme that they name: `counts`: each partition has between 24 and 48 live elements in its first slots; some partition has exactly 48. `face_rows`: each list of a partition holds 2048 distinct node rows of its live elements; its list 0 includes its last live node row.
All inputs are finite; a program needn't handle non-finite values.
Results may differ from the reference program's by a relative error of at most 0.0034.
Values may be sent and summed in bfloat16 or wider, within the bound.
No kernel may reach another device: no remote copies, remote signals or barrier semaphores. Data moves between devices by JAX's collectives and lax.ppermute only.
A program may use at most 128 MiB of HBM per device.

```python
import math
import jax
import jax.numpy as jnp
from jax import lax

NODES = 512
SNAP = 128
RES = 1024
FACE_N = 2048
EL_CAP = 48
PARTITIONS = 32


def layout(key):
    base = jax.random.randint(jax.random.fold_in(key, 11), (PARTITIONS,), EL_CAP // 2, EL_CAP + 1)
    filled = jax.random.randint(jax.random.fold_in(key, 12), (), 0, PARTITIONS)
    counts = jnp.where(jnp.arange(PARTITIONS) == filled, EL_CAP, base).astype(jnp.int32)
    total_rows = EL_CAP * NODES
    position = jnp.arange(total_rows, dtype=jnp.int32)

    def lists(subkey, count):
        score = jax.random.randint(subkey, (2, total_rows), 0, 32768) * 32768 + position[None, :]
        last_live = (position[None, :] == count * NODES - 1) & (jnp.arange(2, dtype=jnp.int32)[:, None] == 0)
        score = jnp.where(last_live, -1, score)
        score = jnp.where(position[None, :] < count * NODES, score, score + 2 ** 30)
        order = jnp.argsort(score, axis=1, stable=True)
        return order[:, :FACE_N].astype(jnp.int32)
    subkeys = jax.random.split(jax.random.fold_in(key, 13), PARTITIONS)
    return (counts, jax.vmap(lists)(subkeys, counts))


def draw_counts(key, part):
    return layout(key)[0]


def draw_face_rows(key, part):
    return layout(key)[1]


def spiked(array, key, source, target, parts, factor):
    def block_of(dim):
        return (jnp.arange(array.shape[dim]) // (array.shape[dim] // parts)).reshape((-1,) + (1,) * (array.ndim - 1 - dim))

    near = jax.random.permutation(key, parts)[block_of(target)]
    far = (block_of(target) + parts // 2) % parts
    return jnp.where((block_of(source) == near) | (block_of(source) == far), factor * array, array)


def block_scale(own_key, dims, pieces, least, top_value):
    level = 1.0
    for dim, shards_of in pieces:
        draws = jax.random.uniform(jax.random.fold_in(jax.random.fold_in(own_key, 6), dim), (shards_of,), jnp.float32, least / len(pieces), top_value / len(pieces))
        level = level * jnp.repeat(jnp.exp(draws), dims[dim] // shards_of).reshape((-1,) + (1,) * (len(dims) - 1 - dim))
    return level


def gaussian(stream_key, shape, spread, limit, pieces=(), held_as=jnp.bfloat16):
    gain = block_scale(stream_key, shape, pieces, -0.22, 0.18) if pieces else 1.0
    drawn = jax.random.normal(stream_key, shape, jnp.float32) * spread * gain
    return jnp.minimum(jnp.maximum(drawn, -limit), limit).astype(held_as)


def heavy_noise(rng, shape, spread, limit, shards, heavy, kind=jnp.bfloat16):
    drawn = spread * jax.random.normal(rng, shape, jnp.float32)
    if shards:
        drawn = drawn * block_scale(rng, shape, shards, -0.22, 0.18)
    return jnp.clip(spiked(drawn, jax.random.fold_in(rng, 3), *heavy), -limit, limit).astype(kind)


def setup_inputs(seed: int = 0) -> dict:
    streams_of = jax.random.split(jax.random.key(seed), 7)
    panel = gaussian(streams_of[0], (PARTITIONS, EL_CAP, NODES, SNAP), 1.0, 6.0, ((0, 32), (1, 4)))
    stiffness = gaussian(streams_of[1], (PARTITIONS, EL_CAP, NODES, NODES), NODES ** -0.5, 0.25, ((0, 32), (1, 4)))
    mass = jnp.clip(jnp.exp(math.log(2.0) - 2.3025851 * jax.random.uniform(streams_of[2], (PARTITIONS, EL_CAP, NODES), jnp.float32) ** block_scale(streams_of[2], (PARTITIONS, EL_CAP, NODES), ((0, 32), (1, 4)), -0.2, 0.2)), 0.2, 2.0)
    resident = heavy_noise(streams_of[3], (PARTITIONS, EL_CAP * NODES, RES), (PARTITIONS * EL_CAP * NODES) ** -0.5, 0.013671875, ((0, 32), (2, 4)), (0, 2, 32, 2.75))
    face_rows = draw_face_rows(jax.random.fold_in(streams_of[6], 71), 0)
    counts = draw_counts(jax.random.fold_in(streams_of[6], 71), 0)
    return {"panel": panel, "stiffness": stiffness, "mass": mass, "resident": resident, "face_rows": face_rows, "counts": counts}


def apply_one(items):
    block, values, weights = items
    values = values.astype(jnp.float32)
    product = jnp.einsum("enm,ems->ens", block.astype(jnp.float32), values)
    return product + weights[:, :, None] * values


def add_faces(values, rows, from_next, from_prev):
    return values.at[rows[1]].add(from_next).at[rows[0]].add(from_prev)


def reference(panel, stiffness, mass, resident, face_rows, counts):
    applied = lax.map(apply_one, (stiffness, panel, mass))
    live = jnp.arange(EL_CAP, dtype=jnp.int32)[None, :] < counts[:, None]
    applied = jnp.where(live[:, :, None, None], applied, 0.0).astype(jnp.bfloat16)
    applied = applied.reshape(PARTITIONS, EL_CAP * NODES, SNAP)
    tiles = jax.vmap(lambda w, idx: w[idx])(applied, face_rows)
    blank = jnp.zeros((1, FACE_N, SNAP), jnp.bfloat16)
    from_next = jnp.concatenate([tiles[1:, 0], blank], axis=0).astype(jnp.float32)
    from_prev = jnp.concatenate([blank, tiles[:-1, 1]], axis=0).astype(jnp.float32)
    summed = jax.vmap(add_faces)(applied.astype(jnp.float32), face_rows, from_next, from_prev)
    summed = summed.astype(jnp.bfloat16)

    def step(total, items):
        left, right = items
        return total + jnp.dot(left.T, right, preferred_element_type=jnp.float32), None

    start = jnp.zeros((RES, SNAP), jnp.float32)
    gram, unused = lax.scan(step, start, (resident, summed))
    return gram
```

```python
import jax
import jax.numpy as jnp
from jax import lax
from jax.sharding import PartitionSpec as P


def passed_along(value, axis, steps):
    count = lax.axis_size(axis)
    leading, last = (max(0, -steps), min(count, count - steps))
    return lax.ppermute(value, axis, [(source, source + steps) for source in range(leading, last)])


def shards(panel, stiffness, mass, resident, face_rows, counts):
    slots = panel.shape[1]
    nodes = panel.shape[2]
    width = panel.shape[3]
    column = lax.axis_index("col")
    slot_ids = column * slots + jnp.arange(slots, dtype=jnp.int32)
    live = slot_ids < counts[0]
    values = panel[0]
    applied = jnp.einsum("enm,ems->ens", stiffness[0], values, preferred_element_type=jnp.float32)
    applied = applied + mass[0][:, :, None] * values.astype(jnp.float32)
    applied = jnp.where(live[:, None, None], applied, 0.0).astype(jnp.bfloat16)
    local_rows = applied.reshape(slots * nodes, width)
    whole = lax.all_gather(local_rows, "col", axis=0, tiled=True)
    prev_rows = face_rows[0, 0]
    next_rows = face_rows[0, 1]
    from_next = passed_along(whole[prev_rows], "row", -1)
    from_prev = passed_along(whole[next_rows], "row", 1)
    summed = whole.astype(jnp.float32)
    summed = summed.at[next_rows].add(from_next.astype(jnp.float32))
    summed = summed.at[prev_rows].add(from_prev.astype(jnp.float32))
    summed = summed.astype(jnp.bfloat16)
    columns = resident[0]
    contract = (((0,), (0,)), ((), ()))
    own_rows = columns.shape[1] // lax.axis_size("row")
    partial_gram = lax.dot_general(columns, summed, contract, preferred_element_type=jnp.float32)
    tiles = partial_gram.reshape(lax.axis_size("row"), own_rows, width)
    received = lax.all_to_all(tiles, "row", 0, 0)
    gram = jnp.sum(received, axis=0)
    return gram


def solution(mesh):
    in_specs = (
        P("row", "col", None, None),
        P("row", "col", None, None),
        P("row", "col", None),
        P("row", None, "col"),
        P("row", None, None),
        P("row"),
    )
    out_specs = P(("col", "row"), None)
    return jax.shard_map(shards, mesh=mesh, in_specs=in_specs, out_specs=out_specs, check_vma=False)
```

```python
import functools

import jax
import jax.numpy as jnp
from jax import lax
from jax.experimental import pallas as pl
from jax.experimental.pallas import tpu as pltpu
from jax.sharding import PartitionSpec as P

CHUNKS = 4
LINE = 4
MIB = 1024 * 1024
ROWS0 = (((0,), (0,)), ((), ()))


def params(mib):
    return pltpu.CompilerParams(vmem_limit_bytes=mib * MIB)


def apply_kernel(first, live_ref, block_ref, values_ref, mass_ref, out_ref):
    slot = first + pl.program_id(0)
    values = values_ref[0]
    product = jnp.dot(block_ref[0], values, preferred_element_type=jnp.float32)
    nodes, width = values.shape
    weights = jnp.broadcast_to(mass_ref[pl.ds(slot, 1), :], (width, nodes)).T
    product = product + weights * values.astype(jnp.float32)
    out_ref[...] = jnp.where(slot < live_ref[0], product, 0.0).astype(jnp.bfloat16)


def apply_chunk(live, stiffness, panel, mass, first, count):
    nodes, width = panel.shape[1:]
    return pl.pallas_call(
        functools.partial(apply_kernel, first),
        grid_spec=pltpu.PrefetchScalarGridSpec(
            num_scalar_prefetch=1,
            grid=(count,),
            in_specs=[
                pl.BlockSpec((1, nodes, nodes), lambda i, s: (first + i, 0, 0)),
                pl.BlockSpec((1, nodes, width), lambda i, s: (first + i, 0, 0)),
                pl.BlockSpec(mass.shape, lambda i, s: (0, 0)),
            ],
            out_specs=pl.BlockSpec((nodes, width), lambda i, s: (i, 0)),
        ),
        out_shape=jax.ShapeDtypeStruct((count * nodes, width), jnp.bfloat16),
        compiler_params=params(16),
        cost_estimate=pl.CostEstimate(
            flops=2 * count * nodes * nodes * width,
            bytes_accessed=2 * count * nodes * (nodes + 2 * width),
            transcendentals=0,
        ),
        name="apply",
    )(live, stiffness, panel, mass)


def take_rows(rows_ref, table_ref, out_ref, count, start=0):
    group = 16

    def body(step, carry):
        base = pl.multiple_of(step * group, group)
        loaded = [table_ref[pl.ds(rows_ref[start + base + j], 1), :] for j in range(group)]
        out_ref[pl.ds(base, group), :] = jnp.concatenate(loaded, axis=0)
        return carry

    lax.fori_loop(0, count // group, body, 0)


def pick_kernel(steps, rows_ref, in_ref, prev_ref, next_ref, table, taken):
    step = pl.program_id(0)
    size = in_ref.shape[0]
    table[pl.ds(pl.multiple_of(step * size, size), size), :] = in_ref[...].astype(jnp.float32)

    @pl.when(step == steps - 1)
    def _():
        count = taken.shape[0]
        take_rows(rows_ref, table, taken, count)
        prev_ref[...] = taken[...].astype(jnp.bfloat16)
        take_rows(rows_ref, table, taken, count, count)
        next_ref[...] = taken[...].astype(jnp.bfloat16)


def pick_resident(lists, resident):
    total, width = resident.shape
    count = lists.shape[0] // 2
    steps = 8
    return pl.pallas_call(
        functools.partial(pick_kernel, steps),
        grid_spec=pltpu.PrefetchScalarGridSpec(
            num_scalar_prefetch=1,
            grid=(steps,),
            in_specs=[pl.BlockSpec((total // steps, width), lambda i, s: (i, 0))],
            out_specs=[pl.BlockSpec((count, width), lambda i, s: (0, 0))] * 2,
            scratch_shapes=[pltpu.VMEM((total, width), jnp.float32), pltpu.VMEM((count, width), jnp.float32)],
        ),
        out_shape=[jax.ShapeDtypeStruct((count, width), jnp.bfloat16)] * 2,
        compiler_params=params(48),
        cost_estimate=pl.CostEstimate(flops=0, bytes_accessed=2 * total * width * 2, transcendentals=0),
        name="pick_resident",
    )(lists, resident)


def edge_kernel(pieces, rows_ref, place_ref, *refs):
    ins, out_ref, table, taken = refs[:pieces], refs[pieces], refs[pieces + 1], refs[pieces + 2]
    size = ins[0].shape[0]
    for j in range(pieces):
        table[pl.ds(pl.multiple_of(place_ref[j] * size, size), size), :] = ins[j][...].astype(jnp.float32)
    table[pl.ds(pieces * size, 8), :] = jnp.zeros((8, table.shape[1]), jnp.float32)
    take_rows(rows_ref, table, taken, taken.shape[0])
    out_ref[...] = taken[...].astype(jnp.bfloat16)


def pick_edge(rows, places, pieces):
    size, width = pieces[0].shape
    count = rows.shape[0]
    return pl.pallas_call(
        functools.partial(edge_kernel, len(pieces)),
        grid_spec=pltpu.PrefetchScalarGridSpec(
            num_scalar_prefetch=2,
            grid=(1,),
            in_specs=[pl.BlockSpec((size, width), lambda i, s, t: (0, 0))] * len(pieces),
            out_specs=pl.BlockSpec((count, width), lambda i, s, t: (0, 0)),
            scratch_shapes=[
                pltpu.VMEM((len(pieces) * size + 8, width), jnp.float32),
                pltpu.VMEM((count, width), jnp.float32),
            ],
        ),
        out_shape=jax.ShapeDtypeStruct((count, width), jnp.bfloat16),
        compiler_params=params(24),
        cost_estimate=pl.CostEstimate(flops=0, bytes_accessed=4 * len(pieces) * size * width, transcendentals=0),
        name="pick_edge",
    )(rows, places, *pieces)


def gram_kernel(pieces, place_ref, left_ref, *refs):
    ins, total_ref, out_ref = refs[:pieces], refs[pieces], refs[pieces + 1]
    step = pl.program_id(0)

    @pl.when(step == 0)
    def _():
        out_ref[...] = total_ref[...]

    for j in range(pieces):

        @pl.when(step == j)
        def _(j=j):
            out_ref[...] += lax.dot_general(left_ref[...], ins[j][...], ROWS0, preferred_element_type=jnp.float32)


def gram_of(places, resident, pieces, total):
    size, width = pieces[0].shape
    columns = resident.shape[1]
    return pl.pallas_call(
        functools.partial(gram_kernel, len(pieces)),
        grid_spec=pltpu.PrefetchScalarGridSpec(
            num_scalar_prefetch=1,
            grid=(len(pieces),),
            in_specs=[pl.BlockSpec((size, columns), lambda i, s: (s[i], 0))]
            + [pl.BlockSpec((size, width), lambda i, s: (0, 0))] * len(pieces)
            + [pl.BlockSpec((columns, width), lambda i, s: (0, 0))],
            out_specs=pl.BlockSpec((columns, width), lambda i, s: (0, 0)),
        ),
        out_shape=jax.ShapeDtypeStruct((columns, width), jnp.float32),
        compiler_params=params(24),
        cost_estimate=pl.CostEstimate(
            flops=2 * len(pieces) * size * columns * width,
            bytes_accessed=2 * len(pieces) * size * (columns + width),
            transcendentals=0,
        ),
        name="gram_of",
    )(places, resident, *pieces, total)


def last_kernel(pieces, late, rows_ref, place_ref, left_ref, prev_ref, next_ref, total_ref, *refs):
    ins, out_ref, table, taken = refs[:pieces], refs[pieces], refs[pieces + 1], refs[pieces + 2]
    step = pl.program_id(0)
    size = ins[0].shape[0]
    count = taken.shape[0]

    @pl.when(step == 0)
    def _():
        for j in range(pieces):
            table[pl.ds(pl.multiple_of(place_ref[j] * size, size), size), :] = ins[j][...].astype(jnp.float32)
        take_rows(rows_ref, table, taken, count)
        got = taken[...].astype(jnp.bfloat16)
        out_ref[...] = total_ref[...] + lax.dot_general(prev_ref[...], got, ROWS0, preferred_element_type=jnp.float32)
        take_rows(rows_ref, table, taken, count, count)
        got = taken[...].astype(jnp.bfloat16)
        out_ref[...] += lax.dot_general(next_ref[...], got, ROWS0, preferred_element_type=jnp.float32)

    for j in range(late):

        @pl.when(step == j)
        def _(j=j):
            out_ref[...] += lax.dot_general(left_ref[...], ins[j][...], ROWS0, preferred_element_type=jnp.float32)


def gram_last(lists, places, resident, from_prev, from_next, total, pieces, late):
    size, width = pieces[0].shape
    columns = resident.shape[1]
    count = lists.shape[0] // 2
    whole = lambda shape: pl.BlockSpec(shape, lambda i, s, t: (0, 0))
    return pl.pallas_call(
        functools.partial(last_kernel, len(pieces), late),
        grid_spec=pltpu.PrefetchScalarGridSpec(
            num_scalar_prefetch=2,
            grid=(late,),
            in_specs=[
                pl.BlockSpec((size, columns), lambda i, s, t: (t[i], 0)),
                whole((count, columns)),
                whole((count, columns)),
                whole((columns, width)),
            ]
            + [whole((size, width))] * len(pieces),
            out_specs=whole((columns, width)),
            scratch_shapes=[
                pltpu.VMEM((len(pieces) * size, width), jnp.float32),
                pltpu.VMEM((count, width), jnp.float32),
            ],
        ),
        out_shape=jax.ShapeDtypeStruct((columns, width), jnp.float32),
        compiler_params=params(44),
        cost_estimate=pl.CostEstimate(
            flops=2 * (late * size + 2 * count) * columns * width,
            bytes_accessed=2 * (len(pieces) * size * width + 2 * count * columns),
            transcendentals=0,
        ),
        name="gram_last",
    )(lists, places, resident, from_prev, from_next, total, *pieces)


def shards(panel, stiffness, mass, resident, face_rows, counts):
    slots, nodes, width = panel.shape[1:]
    cols, rows = lax.axis_size("col"), lax.axis_size("row")
    column, row = lax.axis_index("col"), lax.axis_index("row")
    both = ("col", "row")
    resident = resident[0]
    columns = resident.shape[1]
    lists = face_rows[0].reshape(-1)
    count = lists.shape[0] // 2
    size = slots * nodes // CHUNKS

    def permute(value, move):
        pairs = []
        for source in range(cols * rows):
            target = move(*divmod(source, rows))
            if target is not None:
                pairs.append((source, target[0] * rows + target[1]))
        return lax.ppermute(value, both, pairs)

    across = lambda value: permute(value, lambda c, r: (c ^ 2, r))
    sibling = lambda value: permute(value, lambda c, r: (c ^ 1, r))

    live = (counts - column * slots).astype(jnp.int32)
    per = slots // CHUNKS
    own = [apply_chunk(live, stiffness[0], panel[0], mass[0], k * per, per) for k in range(CHUNKS)]
    far = [across(piece) for piece in own]
    mate = [sibling(piece) for piece in own]
    far_mate = [sibling(piece) for piece in far]

    prev_out, next_out = pick_resident(lists, resident)
    from_prev = permute(next_out, lambda c, r: (c, r + 1) if r % LINE != LINE - 1 else None)
    from_next = permute(prev_out, lambda c, r: (c, r - 1) if r % LINE != 0 else None)

    first = row % LINE == 0
    half = count // 2
    edge_rows = jnp.where(first, face_rows[0, 0], face_rows[0, 1])
    edge_rows = lax.dynamic_slice_in_dim(edge_rows, (column % 2) * half, half, 0)
    edge_rows = edge_rows - (column // 2) * (2 * slots * nodes)
    edge_rows = jnp.where((edge_rows >= 0) & (edge_rows < 2 * slots * nodes), edge_rows, 2 * slots * nodes)
    steps = jnp.arange(CHUNKS, dtype=jnp.int32)
    place = lambda c: c * CHUNKS + steps
    core = column % 2
    edge = pick_edge(edge_rows, jnp.concatenate([place(core), place(1 - core)]), own + mate)

    def beside(c, r):
        if r % LINE == LINE - 1 and r + 1 < rows:
            return c, r + 1
        if r % LINE == 0 and r > 0:
            return c, r - 1
        return None

    def crossed(c, r):
        target = beside(c, r)
        return target if target is None else (target[0] ^ 2, target[1])

    met = permute(edge, beside) + permute(edge, crossed)
    other = sibling(met)
    meeting = jnp.where(first, prev_out, next_out)
    front, back = meeting[:half], meeting[half:]
    mine = jnp.where(core == 0, front, back)
    theirs = jnp.where(core == 0, back, front)
    dot = lambda a, b: lax.dot_general(a, b, ROWS0, preferred_element_type=jnp.float32)
    total = dot(mine, met) + dot(theirs, other)

    total = gram_of(jnp.concatenate([place(column), place(column ^ 1)]), resident, own + mate, total)
    for k in range(CHUNKS - 1):
        here = jnp.stack([(column ^ 2) * CHUNKS + k, (column ^ 3) * CHUNKS + k])
        total = gram_of(here, resident, [far[k], far_mate[k]], total)
    k = CHUNKS - 1
    order = jnp.stack([(column ^ 2) * CHUNKS + k, (column ^ 3) * CHUNKS + k])
    order = jnp.concatenate([order, place(column ^ 2)[:k], place(column ^ 3)[:k], place(column), place(column ^ 1)])
    pieces = [far[k], far_mate[k]] + far[:k] + far_mate[:k] + own + mate
    gram = gram_last(lists, order, resident, from_prev, from_next, total, pieces, 2)

    own_rows = columns // rows
    received = lax.all_to_all(gram.reshape(rows, own_rows, width), "row", 0, 0)
    return jnp.sum(received, axis=0)


def solution(mesh):
    in_specs = (
        P("row", "col", None, None),
        P("row", "col", None, None),
        P("row", "col", None),
        P("row", None, "col"),
        P("row", None, None),
        P("row"),
    )
    out_specs = P(("col", "row"), None)
    return jax.shard_map(shards, mesh=mesh, in_specs=in_specs, out_specs=out_specs, check_vma=False)
```

```python
import functools
import math

import jax
import jax.numpy as jnp
from jax import lax
from jax.experimental import pallas as pl
from jax.experimental.pallas import tpu as pltpu
from jax.sharding import PartitionSpec as P

SPLIT = (3, 1)
LINE = 4
MIB = 1024 * 1024
ROWS0 = (((0,), (0,)), ((), ()))
AXES = ("col", "row")


def params(mib):
    return pltpu.CompilerParams(vmem_limit_bytes=mib * MIB)


HBM = pl.BlockSpec(memory_space=pltpu.HBM)
ANY = pl.BlockSpec(memory_space=pl.ANY)
SMEM = pl.BlockSpec(memory_space=pltpu.SMEM)
VMEM = pl.BlockSpec(memory_space=pltpu.VMEM)


def cost(flops, moved):
    return pl.CostEstimate(flops=flops, bytes_accessed=moved, transcendentals=0)


def in_hbm(value):
    return pltpu.with_memory_space_constraint(value, pltpu.HBM)


def dot0(left, right):
    return lax.dot_general(left, right, ROWS0, preferred_element_type=jnp.float32)


def take_rows(row_of, table_ref, out_ref, count, group=16):
    def body(step, carry):
        base = pl.multiple_of(step * group, group)
        loaded = [table_ref[pl.ds(row_of(base + j), 1), :] for j in range(group)]
        out_ref[pl.ds(base, group), :] = jnp.concatenate(loaded, axis=0)
        return carry

    lax.fori_loop(0, count // group, body, 0)


def widen(table, start, ref):
    size = ref.shape[0]
    table[pl.ds(pl.multiple_of(start, 256), size), :] = ref[...].astype(jnp.float32)


def apply_kernel(first, counts_ref, blocks_ref, values_ref, mass_ref, *refs):
    out_ref, blocks, values, mass, sems = refs[-5:]
    count, nodes, width = values.shape
    slots = values_ref.shape[0]
    copies = [
        (
            pltpu.make_async_copy(blocks_ref.at[first + e], blocks.at[e], sems.at[0, e]),
            pltpu.make_async_copy(values_ref.at[first + e], values.at[e], sems.at[1, e]),
        )
        for e in range(count)
    ]
    weighing = pltpu.make_async_copy(mass_ref.at[pl.ds(first, count)], mass, sems.at[2, 0])
    weighing.start()
    for pair in copies:
        for copy in pair:
            copy.start()
    weighing.wait()
    live = counts_ref[0] - lax.axis_index("col") * slots - first
    for e, pair in enumerate(copies):
        for copy in pair:
            copy.wait()
        value = values[e]
        product = jnp.dot(blocks[e], value, preferred_element_type=jnp.float32)
        weights = jnp.broadcast_to(mass[e], (width, nodes)).T
        product = product + weights * value.astype(jnp.float32)
        out_ref[pl.ds(e * nodes, nodes), :] = jnp.where(e < live, product, 0.0).astype(jnp.bfloat16)


def apply_chunk(counts, stiffness, panel, mass, first, count, earlier):
    nodes, width = panel.shape[1:]
    return pl.pallas_call(
        functools.partial(apply_kernel, first),
        in_specs=[SMEM, HBM, HBM, HBM] + [ANY] * len(earlier),
        out_specs=VMEM,
        out_shape=jax.ShapeDtypeStruct((count * nodes, width), jnp.bfloat16),
        scratch_shapes=[
            pltpu.VMEM((count, nodes, nodes), jnp.bfloat16),
            pltpu.VMEM((count, nodes, width), jnp.bfloat16),
            pltpu.VMEM((count, 1, nodes), jnp.float32),
            pltpu.SemaphoreType.DMA((3, count)),
        ],
        compiler_params=params(12),
        cost_estimate=cost(2 * count * nodes * nodes * width, 2 * count * nodes * (nodes + 2 * width)),
        name="apply",
    )(counts, in_hbm(stiffness), in_hbm(panel), in_hbm(mass), *earlier)


def pick_kernel(steps, rows_ref, in_ref, prev_ref, next_ref, held, table, taken, sems):
    size = held.shape[1]
    copies = [
        pltpu.make_async_copy(in_ref.at[pl.ds(j * size, size)], held.at[j], sems.at[j]) for j in range(steps)
    ]
    for copy in copies:
        copy.start()
    for j, copy in enumerate(copies):
        copy.wait()
        widen(table, j * size, held.at[j])
    count = taken.shape[0]
    take_rows(lambda i: rows_ref[i], table, taken, count, 32)
    prev_ref[...] = taken[...].astype(jnp.bfloat16)
    take_rows(lambda i: rows_ref[count + i], table, taken, count, 32)
    next_ref[...] = taken[...].astype(jnp.bfloat16)


def pick_resident(lists, resident):
    total, width = resident.shape
    count = lists.shape[0] // 2
    steps = 8
    return pl.pallas_call(
        functools.partial(pick_kernel, steps),
        in_specs=[SMEM, HBM],
        out_specs=[VMEM] * 2,
        scratch_shapes=[
            pltpu.VMEM((steps, total // steps, width), jnp.bfloat16),
            pltpu.VMEM((total, width), jnp.float32),
            pltpu.VMEM((count, width), jnp.float32),
            pltpu.SemaphoreType.DMA((steps,)),
        ],
        out_shape=[jax.ShapeDtypeStruct((count, width), jnp.bfloat16)] * 2,
        compiler_params=params(44),
        cost_estimate=cost(0, 4 * total * width),
        name="pick_resident",
    )(lists, in_hbm(resident))


def edge_kernel(places, rows_ref, *refs):
    pieces = len(places)
    ins, (out_ref, last_ref, table, taken) = refs[:pieces], refs[-4:]
    last_ref[...] = ins[pieces // 2 - 1][...]
    span = table.shape[0] - 8
    core = lax.axis_index("col") % 2
    for (flip, offset), ref in zip(places, ins):
        widen(table, (core ^ flip) * (span // 2) + offset, ref)
    table[pl.ds(span, 8), :] = jnp.zeros((8, table.shape[1]), jnp.float32)
    take_rows(lambda i: rows_ref[i], table, taken, taken.shape[0])
    out_ref[...] = taken[...].astype(jnp.bfloat16)


def pick_edge(rows, pieces, places, span, *earlier):
    last = pieces[len(pieces) // 2 - 1]
    width = pieces[0].shape[1]
    count = rows.shape[0]
    return pl.pallas_call(
        functools.partial(edge_kernel, places),
        in_specs=[SMEM] + [VMEM] * len(pieces) + [ANY] * len(earlier),
        out_specs=[VMEM, VMEM],
        scratch_shapes=[pltpu.VMEM((span + 8, width), jnp.float32), pltpu.VMEM((count, width), jnp.float32)],
        out_shape=[jax.ShapeDtypeStruct(shape, jnp.bfloat16) for shape in ((count, width), last.shape)],
        compiler_params=params(16),
        cost_estimate=cost(0, 8 * span * width),
        name="pick_edge",
    )(rows, *pieces, *earlier)


def hold_kernel(parts, in_ref, *refs):
    size = in_ref.shape[0] // parts
    for j, out_ref in enumerate(refs[-parts:]):
        out_ref[...] = in_ref[pl.ds(j * size, size), :]


def hold(value, parts, *earlier):
    shape = (value.shape[0] // parts, value.shape[1])
    return pl.pallas_call(
        functools.partial(hold_kernel, parts),
        in_specs=[VMEM] + [ANY] * len(earlier),
        out_specs=[VMEM] * parts,
        out_shape=[jax.ShapeDtypeStruct(shape, value.dtype)] * parts,
        compiler_params=params(8),
        cost_estimate=cost(0, 4 * value.size),
        name="hold",
    )(value, *earlier)


def edge_gram_kernel(prev_ref, next_ref, mine_ref, other_ref, total_ref, out_ref):
    half = mine_ref.shape[0]
    core = lax.axis_index("col") % 2
    mine = pl.ds(pl.multiple_of(core * half, half), half)
    other = pl.ds(pl.multiple_of((1 - core) * half, half), half)
    first = lax.axis_index("row") % LINE == 0

    @pl.when(first)
    def _():
        out_ref[...] = total_ref[...] + dot0(prev_ref[mine, :], mine_ref[...]) + dot0(prev_ref[other, :], other_ref[...])

    @pl.when(jnp.logical_not(first))
    def _():
        out_ref[...] = total_ref[...] + dot0(next_ref[mine, :], mine_ref[...]) + dot0(next_ref[other, :], other_ref[...])


def edge_gram(prev_out, next_out, mine, other, total):
    arrays = (prev_out, next_out, mine, other, total)
    return pl.pallas_call(
        edge_gram_kernel,
        in_specs=[VMEM] * len(arrays),
        out_specs=VMEM,
        out_shape=jax.ShapeDtypeStruct(total.shape, jnp.float32),
        compiler_params=params(8),
        cost_estimate=cost(2 * prev_out.size * mine.shape[1], 4 * prev_out.size),
        name="edge_gram",
    )(*arrays)


def gram_steps(places, left_ref, ins, held, sems):
    slots, size = held.shape[:2]
    column = lax.axis_index("col")
    share = left_ref.shape[0] // lax.axis_size("col")
    blocks = [
        (flip, offset + start, ref, start)
        for (flip, offset), ref in zip(places, ins)
        for start in range(0, ref.shape[0], size)
    ]

    def copy(j):
        flip, offset = blocks[j][:2]
        start = pl.multiple_of((column ^ flip) * share + offset, 256)
        return pltpu.make_async_copy(left_ref.at[pl.ds(start, size)], held.at[j % slots], sems.at[j % slots])

    def begin():
        for j in range(min(slots, len(blocks))):
            copy(j).start()

    def finish(total):
        for j, (_, _, ref, start) in enumerate(blocks):
            copy(j).wait()
            product = dot0(held[j % slots], ref[pl.ds(start, size), :])
            total = product if total is None else total + product
            if j + slots < len(blocks):
                copy(j + slots).start()
        return total

    return begin, finish


def gram_kernel(places, has_total, left_ref, *refs):
    count = len(places)
    held, sems = refs[-2:]
    begin, finish = gram_steps(places, left_ref, refs[:count], held, sems)
    begin()
    refs[-3][...] = finish(refs[count][...] if has_total else None)


def gram_of(resident, pieces, places, total=None, earlier=()):
    width = pieces[0].shape[1]
    columns = resident.shape[1]
    slots, block = 4, math.gcd(*(piece.shape[0] for piece in pieces))
    height = sum(piece.shape[0] for piece in pieces)
    return pl.pallas_call(
        functools.partial(gram_kernel, places, total is not None),
        in_specs=[HBM] + [VMEM] * (len(pieces) + (total is not None)) + [ANY] * len(earlier),
        out_specs=VMEM,
        out_shape=jax.ShapeDtypeStruct((columns, width), jnp.float32),
        scratch_shapes=[
            pltpu.VMEM((slots, block, columns), jnp.bfloat16),
            pltpu.SemaphoreType.DMA((slots,)),
        ],
        compiler_params=params(16),
        cost_estimate=cost(2 * height * columns * width, 2 * height * (columns + width)),
        name="gram_of",
    )(in_hbm(resident), *pieces, *([] if total is None else [total]), *earlier)


def early_kernel(places, rows_ref, *refs):
    pieces = len(places)
    ins, out_ref, table, taken = refs[:pieces], refs[pieces], refs[pieces + 1], refs[pieces + 2]
    column = lax.axis_index("col")
    share = table.shape[0] // lax.axis_size("col")
    for (flip, offset), ref in zip(places, ins):
        widen(table, (column ^ flip) * share + offset, ref)
    size = share - ins[0].shape[0]
    for flip in (2, 3):
        late = pl.multiple_of((column ^ flip) * share + share - size, 512)
        table[pl.ds(late, size), :] = jnp.zeros((size, table.shape[1]), jnp.float32)
    take_rows(lambda i: rows_ref[i], table, taken, taken.shape[0])
    out_ref[...] = taken[...].astype(jnp.bfloat16)


def pick_early(lists, pieces, places, total):
    width = pieces[0].shape[1]
    count = lists.shape[0]
    return pl.pallas_call(
        functools.partial(early_kernel, places),
        in_specs=[SMEM] + [VMEM] * len(pieces),
        out_specs=VMEM,
        scratch_shapes=[pltpu.VMEM((total, width), jnp.float32), pltpu.VMEM((count, width), jnp.float32)],
        out_shape=jax.ShapeDtypeStruct((count, width), jnp.bfloat16),
        compiler_params=params(24),
        cost_estimate=cost(0, 4 * total * width),
        name="pick_early",
    )(lists, *pieces)


def last_kernel(rows_ref, left_ref, prev_ref, next_ref, early_ref, total_ref, far_ref, mate_ref, out_ref, held, table, taken, sems):
    size = far_ref.shape[0]
    count = prev_ref.shape[0]
    share = left_ref.shape[0] // lax.axis_size("col")
    places = ((2, share - size), (3, share - size))
    begin, finish = gram_steps(places, left_ref, (far_ref, mate_ref), held, sems)
    begin()
    table[pl.ds(0, size), :] = far_ref[...].astype(jnp.float32)
    table[pl.ds(size, size), :] = mate_ref[...].astype(jnp.float32)
    table[pl.ds(2 * size, 8), :] = jnp.zeros((8, table.shape[1]), jnp.float32)
    take_rows(lambda i: rows_ref[i], table, taken, 2 * count)
    got = early_ref[...] + taken[...].astype(jnp.bfloat16)
    total = total_ref[...] + dot0(prev_ref[...], got[:count]) + dot0(next_ref[...], got[count:])
    out_ref[...] = finish(total)


def gram_last(rows, resident, from_prev, from_next, early, total, far, mate):
    size, width = far.shape
    columns = resident.shape[1]
    count = rows.shape[0] // 2
    return pl.pallas_call(
        last_kernel,
        in_specs=[SMEM, HBM] + [VMEM] * 6,
        out_specs=VMEM,
        scratch_shapes=[
            pltpu.VMEM((2, size, columns), jnp.bfloat16),
            pltpu.VMEM((2 * size + 8, width), jnp.float32),
            pltpu.VMEM((2 * count, width), jnp.float32),
            pltpu.SemaphoreType.DMA((2,)),
        ],
        out_shape=jax.ShapeDtypeStruct((columns, width), jnp.float32),
        compiler_params=params(24),
        cost_estimate=cost(4 * (size + count) * columns * width, 8 * (size + count) * columns),
        name="gram_last",
    )(rows, in_hbm(resident), from_prev, from_next, early, total, far, mate)


def shards(panel, stiffness, mass, resident, face_rows, counts):
    slots, nodes, width = panel.shape[1:]
    cols, rows = lax.axis_size("col"), lax.axis_size("row")
    resident = resident[0]
    columns = resident.shape[1]
    weights = mass[0].reshape(slots, 1, nodes)

    def permute(value, move):
        pairs = []
        for source in range(cols * rows):
            target = move(*divmod(source, rows))
            if target is not None:
                pairs.append((source, target[0] * rows + target[1]))
        return lax.ppermute(value, AXES, pairs)

    def across(value):
        return permute(value, lambda c, r: (c ^ 2, r))

    def sibling(value):
        return permute(value, lambda c, r: (c ^ 1, r))

    column, row = lax.axis_index("col"), lax.axis_index("row")
    share = slots * nodes
    per = slots // sum(SPLIT)
    pieces, offsets = [], []
    for k, parts in enumerate(SPLIT):
        first = per * sum(SPLIT[:k])
        pieces.append(apply_chunk(counts, stiffness[0], panel[0], weights, first, per * parts, pieces[-1:]))
        offsets.append(first * nodes)
    far = [across(piece) for piece in pieces[:-1]]
    mate = [sibling(piece) for piece in pieces]
    here = [(flip, offset) for flip in (0, 1) for offset in offsets]

    lists = face_rows[0].reshape(-1)
    count = face_rows.shape[2]
    prev_out, next_out = pick_resident(lists, resident)
    from_prev = permute(next_out, lambda c, r: (c, r + 1) if r % LINE != LINE - 1 else None)
    from_next = permute(prev_out, lambda c, r: (c, r - 1) if r % LINE != 0 else None)

    edge_rows = jnp.where(row % LINE == 0, lists[:count], lists[count:])
    half = count // 2
    edge_rows = jnp.where(column % 2 == 0, edge_rows[:half], edge_rows[half:]) - column // 2 * 2 * share
    edge_rows = jnp.where((edge_rows >= 0) & (edge_rows < 2 * share), edge_rows, 2 * share)
    edge, last = pick_edge(edge_rows, pieces + mate, here, 2 * share, prev_out)
    far.append(across(last))

    def beside(c, r):
        if r % LINE == LINE - 1 and r + 1 < rows:
            return c, r + 1
        if r % LINE == 0 and r > 0:
            return c, r - 1
        return None

    def crossed(c, r):
        target = beside(c, r)
        return target if target is None else (target[0] ^ 2, target[1])

    near_half, far_half = permute(edge, beside), permute(edge, crossed)
    met = near_half + far_half
    other = sibling(met)
    parts = 2
    far_mate = [sibling(part) for part in hold(far[0], parts, edge)]
    height = offsets[1] // parts
    arrived = [far[0]] + far_mate
    there = [(2, 0)] + [(3, j * height) for j in range(parts)]
    early = pick_early(lists, pieces + mate + arrived, here + there, resident.shape[0])
    total = gram_of(resident, pieces + mate, here)
    total = gram_of(resident, arrived, there, total, (from_prev, from_next))
    last_mate = sibling(hold(far[1], 1, early, total)[0])
    total = edge_gram(prev_out, next_out, met, other, total)
    size = far[-1].shape[0]
    late_rows = jnp.full_like(lists, 2 * size)
    for j, flip in enumerate((2, 3)):
        found = lists - ((column ^ flip) * share + share - size)
        late_rows = jnp.where((found >= 0) & (found < size), found + j * size, late_rows)
    gram = gram_last(late_rows, resident, from_prev, from_next, early, total, far[-1], last_mate)

    own_rows = columns // rows
    received = lax.all_to_all(gram.reshape(rows, own_rows, width), "row", 0, 0)
    return jnp.sum(received, axis=0)


def solution(mesh):
    in_specs = (
        P("row", "col", None, None),
        P("row", "col", None, None),
        P("row", "col", None),
        P("row", None, "col"),
        P("row", None, None),
        P("row"),
    )
    out_specs = P(("col", "row"), None)
    return jax.shard_map(shards, mesh=mesh, in_specs=in_specs, out_specs=out_specs, check_vma=False)
```

```python
import functools
import math

import jax
import jax.numpy as jnp
from jax import lax
from jax.experimental import pallas as pl
from jax.experimental.pallas import tpu as pltpu
from jax.sharding import PartitionSpec as P

SPLIT = (1, 3)
MIB = 1024 * 1024
ROWS0 = (((0,), (0,)), ((), ()))
AXES = ("col", "row")


def params(mib):
    return pltpu.CompilerParams(vmem_limit_bytes=mib * MIB)


HBM = pl.BlockSpec(memory_space=pltpu.HBM)
ANY = pl.BlockSpec(memory_space=pl.ANY)
SMEM = pl.BlockSpec(memory_space=pltpu.SMEM)
VMEM = pl.BlockSpec(memory_space=pltpu.VMEM)


def cost(flops, moved):
    return pl.CostEstimate(flops=flops, bytes_accessed=moved, transcendentals=0)


def in_hbm(value):
    return pltpu.with_memory_space_constraint(value, pltpu.HBM)


def dot0(left, right):
    return lax.dot_general(left, right, ROWS0, preferred_element_type=jnp.float32)


def take_rows(row_of, table_ref, out_ref, start, count, group=32):
    def body(step, carry):
        base = pl.multiple_of(step * group, group)
        loaded = [table_ref[pl.ds(row_of(base + j), 1), :] for j in range(group)]
        out_ref[pl.ds(start + base, group), :] = jnp.concatenate(loaded, axis=0)
        return carry

    lax.fori_loop(0, count // group, body, 0)


def widen(table, start, ref):
    size = ref.shape[0]
    table[pl.ds(pl.multiple_of(start, 256), size), :] = ref[...].astype(jnp.float32)


def apply_steps(first, counts_ref, blocks_ref, values_ref, mass_ref, out_ref, blocks, values, mass, sems):
    count, nodes, width = values.shape
    slots = values_ref.shape[0]
    copies = [
        (
            pltpu.make_async_copy(blocks_ref.at[first + e], blocks.at[e], sems.at[0, e]),
            pltpu.make_async_copy(values_ref.at[first + e], values.at[e], sems.at[1, e]),
        )
        for e in range(count)
    ]
    weighing = pltpu.make_async_copy(mass_ref.at[pl.ds(first, count)], mass, sems.at[2, 0])

    def begin():
        weighing.start()
        for pair in copies:
            for copy in pair:
                copy.start()

    def finish():
        weighing.wait()
        live = counts_ref[0] - lax.axis_index("col") * slots - first
        for e, pair in enumerate(copies):
            for copy in pair:
                copy.wait()
            value = values[e]
            product = jnp.dot(blocks[e], value, preferred_element_type=jnp.float32)
            weights = jnp.broadcast_to(mass[e], (width, nodes)).T
            product = product + weights * value.astype(jnp.float32)
            out_ref[pl.ds(e * nodes, nodes), :] = jnp.where(e < live, product, 0.0).astype(jnp.bfloat16)

    return begin, finish


def apply_scratch(count, nodes, width):
    return [
        pltpu.VMEM((count, nodes, nodes), jnp.bfloat16),
        pltpu.VMEM((count, nodes, width), jnp.bfloat16),
        pltpu.VMEM((count, 1, nodes), jnp.float32),
        pltpu.SemaphoreType.DMA((3, count)),
    ]


def apply_kernel(first, *refs):
    begin, finish = apply_steps(first, *refs[:4], *refs[-5:])
    begin()
    finish()


def apply_chunk(counts, stiffness, panel, mass, first, count, earlier):
    nodes, width = panel.shape[1:]
    return pl.pallas_call(
        functools.partial(apply_kernel, first),
        in_specs=[SMEM, HBM, HBM, HBM] + [ANY] * len(earlier),
        out_specs=VMEM,
        out_shape=jax.ShapeDtypeStruct((count * nodes, width), jnp.bfloat16),
        scratch_shapes=apply_scratch(count, nodes, width),
        compiler_params=params(12),
        cost_estimate=cost(2 * count * nodes * nodes * width, 2 * count * nodes * (nodes + 2 * width)),
        name="apply",
    )(counts, in_hbm(stiffness), in_hbm(panel), in_hbm(mass), *earlier)


def list_starts(count):
    start = jnp.where(lax.axis_index("row") % 2 == 0, count, 0)
    return start, count - start


def pick_kernel(pieces, rows_ref, in_ref, *refs):
    first_ref, second_ref, low_ref, high_ref, again_ref, held, left, right, left_taken, right_taken, sems = refs[-11:]
    steps, size = held.shape[:2]
    copies = [
        pltpu.make_async_copy(in_ref.at[pl.ds(j * size, size)], held.at[j], sems.at[j]) for j in range(steps)
    ]
    for copy in copies:
        copy.start()
    values = jnp.concatenate([piece[...] for piece in refs[:pieces]], axis=0)
    low_ref[...] = values[: low_ref.shape[0]]
    high_ref[...] = values[low_ref.shape[0] :]
    again_ref[...] = refs[pieces][...]
    lanes = left.shape[1]
    for j, copy in enumerate(copies):
        copy.wait()
        left[pl.ds(j * size, size), :] = held[j, :, :lanes].astype(jnp.float32)
        right[pl.ds(j * size, size), :] = held[j, :, lanes:].astype(jnp.float32)
    count = left_taken.shape[0]
    group = 32
    for begins, out_ref in zip(list_starts(count), (first_ref, second_ref)):

        def body(step, carry):
            base = pl.multiple_of(step * group, group)
            rows = [rows_ref[begins + base + i] for i in range(group)]
            for table, taken in ((left, left_taken), (right, right_taken)):
                taken[pl.ds(base, group), :] = jnp.concatenate([table[pl.ds(row, 1), :] for row in rows], axis=0)
            return carry

        lax.fori_loop(0, count // group, body, 0)
        out_ref[:, :lanes] = left_taken[...].astype(jnp.bfloat16)
        out_ref[:, lanes:] = right_taken[...].astype(jnp.bfloat16)


def pick_resident(lists, resident, pieces, arrived):
    total, columns = resident.shape
    count = lists.shape[0] // 2
    steps, lanes = 8, columns // 2
    height, width = sum(piece.shape[0] for piece in pieces), pieces[0].shape[1]
    return pl.pallas_call(
        functools.partial(pick_kernel, len(pieces)),
        in_specs=[SMEM, HBM] + [VMEM] * (len(pieces) + 1),
        out_specs=[VMEM] * 5,
        scratch_shapes=[
            pltpu.VMEM((steps, total // steps, columns), jnp.bfloat16),
            pltpu.VMEM((total, lanes), jnp.float32),
            pltpu.VMEM((total, lanes), jnp.float32),
            pltpu.VMEM((count, lanes), jnp.float32),
            pltpu.VMEM((count, lanes), jnp.float32),
            pltpu.SemaphoreType.DMA((steps,)),
        ],
        out_shape=[jax.ShapeDtypeStruct((count, columns), jnp.bfloat16)] * 2
        + [jax.ShapeDtypeStruct((height // 2, width), jnp.bfloat16)] * 2
        + [jax.ShapeDtypeStruct(arrived.shape, jnp.bfloat16)],
        compiler_params=params(46),
        cost_estimate=cost(0, 4 * total * columns),
        name="pick_resident",
    )(lists, in_hbm(resident), *pieces, arrived)


def hold_kernel(parts, *refs):
    outs = list(refs[-sum(parts) :])
    for in_ref, count in zip(refs, parts):
        size = in_ref.shape[0] // count
        for j in range(count):
            outs.pop(0)[...] = in_ref[pl.ds(j * size, size), :]


def hold(values, parts, *earlier):
    shapes = [(value.shape[0] // count, value.shape[1]) for value, count in zip(values, parts) for _ in range(count)]
    return pl.pallas_call(
        functools.partial(hold_kernel, parts),
        in_specs=[VMEM] * len(values) + [ANY] * len(earlier),
        out_specs=[VMEM] * len(shapes),
        out_shape=[jax.ShapeDtypeStruct(shape, jnp.bfloat16) for shape in shapes],
        compiler_params=params(12),
        cost_estimate=cost(0, 4 * values[0].size),
        name="hold",
    )(*values, *earlier)


def join_kernel(first_ref, second_ref, _, out_ref):
    size = first_ref.shape[0]
    out_ref[pl.ds(0, size), :] = first_ref[...]
    out_ref[pl.ds(size, size), :] = second_ref[...]


def join(first, second, earlier):
    shape = (2 * first.shape[0], first.shape[1])
    return pl.pallas_call(
        join_kernel,
        in_specs=[VMEM, VMEM, ANY],
        out_specs=VMEM,
        out_shape=jax.ShapeDtypeStruct(shape, first.dtype),
        compiler_params=params(8),
        cost_estimate=cost(0, 8 * first.size),
        name="join",
    )(first, second, earlier)


def gram_steps(places, left_ref, ins, held, sems):
    slots, size = held.shape[:2]
    column = lax.axis_index("col")
    share = left_ref.shape[0] // lax.axis_size("col")
    blocks = [
        (flip, offset + start, ref, start)
        for (flip, offset), ref in zip(places, ins)
        for start in range(0, ref.shape[0], size)
    ]

    def copy(j):
        flip, offset = blocks[j][:2]
        start = pl.multiple_of((column ^ flip) * share + offset, 256)
        return pltpu.make_async_copy(left_ref.at[pl.ds(start, size)], held.at[j % slots], sems.at[j % slots])

    def begin():
        for j in range(min(slots, len(blocks))):
            copy(j).start()

    def finish(total):
        for j, (_, _, ref, start) in enumerate(blocks):
            copy(j).wait()
            product = dot0(ref[pl.ds(start, size), :], held[j % slots])
            total = product if total is None else total + product
            if j + slots < len(blocks):
                copy(j + slots).start()
        return total

    return begin, finish


def gram_kernel(places, has_total, left_ref, *refs):
    count = len(places)
    out_ref, held, sems = refs[-3:]
    begin, finish = gram_steps(places, left_ref, refs[:count], held, sems)
    begin()
    out_ref[...] = finish(refs[count][...] if has_total else None)


def gram_of(resident, pieces, places, total=None, earlier=()):
    width = pieces[0].shape[1]
    columns = resident.shape[1]
    slots, block = 4, math.gcd(2048 * 3072, *(piece.shape[0] for piece in pieces))
    height = sum(piece.shape[0] for piece in pieces)
    return pl.pallas_call(
        functools.partial(gram_kernel, places, total is not None),
        in_specs=[HBM] + [VMEM] * (len(pieces) + (total is not None)) + [ANY] * len(earlier),
        out_specs=VMEM,
        out_shape=jax.ShapeDtypeStruct((width, columns), jnp.float32),
        scratch_shapes=[
            pltpu.VMEM((slots, block, columns), jnp.bfloat16),
            pltpu.SemaphoreType.DMA((slots,)),
        ],
        compiler_params=params(16),
        cost_estimate=cost(2 * height * columns * width, 2 * height * (columns + width)),
        name="gram_of",
    )(in_hbm(resident), *pieces, *([] if total is None else [total]), *earlier)


def tiles_kernel(places, rows_ref, *refs):
    ins, (toward_ref, away_ref, table, taken) = refs[:-4], refs[-4:]
    column = lax.axis_index("col")
    share = table.shape[0] // lax.axis_size("col")
    for (flip, offset), ref in zip(places, ins):
        widen(table, (column ^ flip) * share + offset, ref)
    half = taken.shape[0]
    for begins, out_ref in zip(list_starts(2 * half), (toward_ref, away_ref)):
        start = begins + column % 2 * half
        take_rows(lambda i: rows_ref[start + i], table, taken, 0, half)
        out_ref[...] = taken[...].astype(jnp.bfloat16)


def pick_tiles(lists, pieces, places, total):
    width = pieces[0].shape[1]
    half = lists.shape[0] // 4
    return pl.pallas_call(
        functools.partial(tiles_kernel, places),
        in_specs=[SMEM] + [VMEM] * len(pieces),
        out_specs=[VMEM] * 2,
        scratch_shapes=[pltpu.VMEM((total, width), jnp.float32), pltpu.VMEM((half, width), jnp.float32)],
        out_shape=[jax.ShapeDtypeStruct((half, width), jnp.bfloat16)] * 2,
        compiler_params=params(20),
        cost_estimate=cost(0, 4 * total * width),
        name="pick_tiles",
    )(lists, *pieces)


def finish_kernel(first_ref, second_ref, mine_ref, other_ref, total_ref, out_ref):
    half = mine_ref.shape[0] // 2
    core = lax.axis_index("col") % 2
    total = total_ref[...]
    for j, left in enumerate((first_ref, second_ref)):
        for flip, tiles in enumerate((mine_ref, other_ref)):
            rows = left[pl.ds(pl.multiple_of((core ^ flip) * half, half), half), :]
            total = total + dot0(tiles[pl.ds(j * half, half), :], rows)
    out_ref[...] = total.T


def finish(first, second, mine, other, total):
    arrays = (first, second, mine, other, total)
    return pl.pallas_call(
        finish_kernel,
        in_specs=[VMEM] * len(arrays),
        out_specs=VMEM,
        out_shape=jax.ShapeDtypeStruct(total.shape[::-1], jnp.float32),
        compiler_params=params(12),
        cost_estimate=cost(4 * first.size * mine.shape[1], 4 * first.size),
        name="finish",
    )(*arrays)


def shards(panel, stiffness, mass, resident, face_rows, counts):
    slots, nodes, width = panel.shape[1:]
    cols, rows = lax.axis_size("col"), lax.axis_size("row")
    resident = resident[0]
    columns = resident.shape[1]
    weights = mass[0].reshape(slots, 1, nodes)

    def permute(value, move):
        pairs = []
        for source in range(cols * rows):
            target = move(*divmod(source, rows))
            if target is not None:
                pairs.append((source, target[0] * rows + target[1]))
        return lax.ppermute(value, AXES, pairs)

    def across(value):
        return permute(value, lambda c, r: (c ^ 2, r))

    def sibling(value):
        return permute(value, lambda c, r: (c ^ 1, r))

    column, row = lax.axis_index("col"), lax.axis_index("row")
    share = slots * nodes
    per = slots // sum(SPLIT)
    second = per * SPLIT[0]
    offsets = (0, second * nodes)
    lists = face_rows[0].reshape(-1)
    stiffness, panel = stiffness[0], panel[0]
    pieces, far = [], []
    for first, elements in ((0, second), (second, slots - second)):
        pieces.append(apply_chunk(counts, stiffness, panel, weights, first, elements, pieces))
        far.append(across(pieces[-1]))
    first_rows, second_rows, *own = pick_resident(lists, resident, pieces, far[0])
    pieces = own + [sibling(piece) for piece in own]
    places = [(flip, offset) for flip in (0, 1) for offset in (0, share // 2)]
    places[2:2] = [(2, 0)]
    places.append((3, 0))
    total = gram_of(resident, pieces, places)
    last = [far[1], sibling(hold([far[1]], (1,), total)[0])]
    last_places = [(2, offsets[1]), (3, offsets[1])]

    toward, away = pick_tiles(lists, pieces + last, places + last_places, resident.shape[0])
    total = gram_of(resident, last, last_places, total, (toward,))

    def beside(c, r):
        target = r + 1 if r % 2 else r - 1
        return (c, target) if 0 <= target < rows else None

    mine = join(permute(toward, lambda c, r: (c, r ^ 1)), permute(away, beside), total)
    gram = finish(first_rows, second_rows, mine, sibling(mine), total)

    own_rows = columns // rows
    received = lax.all_to_all(gram.reshape(rows, own_rows, width), "row", 0, 0)
    return jnp.sum(received, axis=0)


def solution(mesh):
    in_specs = (
        P("row", "col", None, None),
        P("row", "col", None, None),
        P("row", "col", None),
        P("row", None, "col"),
        P("row", None, None),
        P("row"),
    )
    out_specs = P(("col", "row"), None)
    return jax.shard_map(shards, mesh=mesh, in_specs=in_specs, out_specs=out_specs, check_vma=False)
```

```python
import functools
import math

import jax
import jax.numpy as jnp
from jax import lax
from jax.experimental import pallas as pl
from jax.experimental.pallas import tpu as pltpu
from jax.sharding import PartitionSpec as P

SPLIT = (1, 3)
MIB = 1024 * 1024
ROWS0 = (((0,), (0,)), ((), ()))
AXES = ("col", "row")


def params(mib):
    return pltpu.CompilerParams(vmem_limit_bytes=mib * MIB)


HBM = pl.BlockSpec(memory_space=pltpu.HBM)
ANY = pl.BlockSpec(memory_space=pl.ANY)
SMEM = pl.BlockSpec(memory_space=pltpu.SMEM)
VMEM = pl.BlockSpec(memory_space=pltpu.VMEM)


def cost(flops, moved):
    return pl.CostEstimate(flops=flops, bytes_accessed=moved, transcendentals=0)


def in_hbm(value):
    return pltpu.with_memory_space_constraint(value, pltpu.HBM)


def dot0(left, right):
    return lax.dot_general(left, right, ROWS0, preferred_element_type=jnp.float32)


def take_rows(row_of, table_ref, out_ref, start, count, group=32):
    def body(step, carry):
        base = pl.multiple_of(step * group, group)
        loaded = [table_ref[pl.ds(row_of(base + j), 1), :] for j in range(group)]
        out_ref[pl.ds(start + base, group), :] = jnp.concatenate(loaded, axis=0)
        return carry

    lax.fori_loop(0, count // group, body, 0)


def widen(table, start, ref):
    size = ref.shape[0]
    table[pl.ds(pl.multiple_of(start, 256), size), :] = ref[...].astype(jnp.float32)


def apply_steps(first, counts_ref, blocks_ref, values_ref, mass_ref, out_ref, blocks, values, mass, sems):
    count, nodes, width = values.shape
    slots = values_ref.shape[0]
    copies = [
        (
            pltpu.make_async_copy(blocks_ref.at[first + e], blocks.at[e], sems.at[0, e]),
            pltpu.make_async_copy(values_ref.at[first + e], values.at[e], sems.at[1, e]),
        )
        for e in range(count)
    ]
    weighing = pltpu.make_async_copy(mass_ref.at[pl.ds(first, count)], mass, sems.at[2, 0])

    def begin():
        weighing.start()
        for pair in copies:
            for copy in pair:
                copy.start()

    def finish():
        weighing.wait()
        live = counts_ref[0] - lax.axis_index("col") * slots - first
        for e, pair in enumerate(copies):
            for copy in pair:
                copy.wait()
            value = values[e]
            product = jnp.dot(blocks[e], value, preferred_element_type=jnp.float32)
            weights = jnp.broadcast_to(mass[e], (width, nodes)).T
            product = product + weights * value.astype(jnp.float32)
            out_ref[pl.ds(e * nodes, nodes), :] = jnp.where(e < live, product, 0.0).astype(jnp.bfloat16)

    return begin, finish


def apply_scratch(count, nodes, width):
    return [
        pltpu.VMEM((count, nodes, nodes), jnp.bfloat16),
        pltpu.VMEM((count, nodes, width), jnp.bfloat16),
        pltpu.VMEM((count, 1, nodes), jnp.float32),
        pltpu.SemaphoreType.DMA((3, count)),
    ]


def apply_kernel(first, *refs):
    begin, finish = apply_steps(first, *refs[:4], *refs[-5:])
    begin()
    finish()


def apply_chunk(counts, stiffness, panel, mass, first, count, earlier):
    nodes, width = panel.shape[1:]
    return pl.pallas_call(
        functools.partial(apply_kernel, first),
        in_specs=[SMEM, HBM, HBM, HBM] + [ANY] * len(earlier),
        out_specs=VMEM,
        out_shape=jax.ShapeDtypeStruct((count * nodes, width), jnp.bfloat16),
        scratch_shapes=apply_scratch(count, nodes, width),
        compiler_params=params(12),
        cost_estimate=cost(2 * count * nodes * nodes * width, 2 * count * nodes * (nodes + 2 * width)),
        name="apply",
    )(counts, in_hbm(stiffness), in_hbm(panel), in_hbm(mass), *earlier)


def list_starts(count):
    start = jnp.where(lax.axis_index("row") % 2 == 0, count, 0)
    return start, count - start


def pick_kernel(pieces, rows_ref, in_ref, *refs):
    first_ref, second_ref, low_ref, high_ref, again_ref, held, left, right, left_taken, right_taken, sems = refs[-11:]
    steps, size = held.shape[:2]
    copies = [
        pltpu.make_async_copy(in_ref.at[pl.ds(j * size, size)], held.at[j], sems.at[j]) for j in range(steps)
    ]
    for copy in copies:
        copy.start()
    values = jnp.concatenate([piece[...] for piece in refs[:pieces]], axis=0)
    low_ref[...] = values[: low_ref.shape[0]]
    high_ref[...] = values[low_ref.shape[0] :]
    again_ref[...] = refs[pieces][...]
    lanes = left.shape[1]
    for j, copy in enumerate(copies):
        copy.wait()
        left[pl.ds(j * size, size), :] = held[j, :, :lanes].astype(jnp.float32)
        right[pl.ds(j * size, size), :] = held[j, :, lanes:].astype(jnp.float32)
    count = left_taken.shape[0]
    group = 32
    for begins, out_ref in zip(list_starts(count), (first_ref, second_ref)):

        def body(step, carry):
            base = pl.multiple_of(step * group, group)
            rows = [rows_ref[begins + base + i] for i in range(group)]
            for table, taken in ((left, left_taken), (right, right_taken)):
                taken[pl.ds(base, group), :] = jnp.concatenate([table[pl.ds(row, 1), :] for row in rows], axis=0)
            return carry

        lax.fori_loop(0, count // group, body, 0)
        out_ref[:, :lanes] = left_taken[...].astype(jnp.bfloat16)
        out_ref[:, lanes:] = right_taken[...].astype(jnp.bfloat16)


def pick_resident(lists, resident, pieces, arrived):
    total, columns = resident.shape
    count = lists.shape[0] // 2
    steps, lanes = 8, columns // 2
    height, width = sum(piece.shape[0] for piece in pieces), pieces[0].shape[1]
    return pl.pallas_call(
        functools.partial(pick_kernel, len(pieces)),
        in_specs=[SMEM, HBM] + [VMEM] * (len(pieces) + 1),
        out_specs=[VMEM] * 5,
        scratch_shapes=[
            pltpu.VMEM((steps, total // steps, columns), jnp.bfloat16),
            pltpu.VMEM((total, lanes), jnp.float32),
            pltpu.VMEM((total, lanes), jnp.float32),
            pltpu.VMEM((count, lanes), jnp.float32),
            pltpu.VMEM((count, lanes), jnp.float32),
            pltpu.SemaphoreType.DMA((steps,)),
        ],
        out_shape=[jax.ShapeDtypeStruct((count, columns), jnp.bfloat16)] * 2
        + [jax.ShapeDtypeStruct((height // 2, width), jnp.bfloat16)] * 2
        + [jax.ShapeDtypeStruct(arrived.shape, jnp.bfloat16)],
        compiler_params=params(46),
        cost_estimate=cost(0, 4 * total * columns),
        name="pick_resident",
    )(lists, in_hbm(resident), *pieces, arrived)


def hold_kernel(parts, *refs):
    outs = list(refs[-sum(parts) :])
    for in_ref, count in zip(refs, parts):
        size = in_ref.shape[0] // count
        for j in range(count):
            outs.pop(0)[...] = in_ref[pl.ds(j * size, size), :]


def hold(values, parts, *earlier):
    shapes = [(value.shape[0] // count, value.shape[1]) for value, count in zip(values, parts) for _ in range(count)]
    return pl.pallas_call(
        functools.partial(hold_kernel, parts),
        in_specs=[VMEM] * len(values) + [ANY] * len(earlier),
        out_specs=[VMEM] * len(shapes),
        out_shape=[jax.ShapeDtypeStruct(shape, jnp.bfloat16) for shape in shapes],
        compiler_params=params(12),
        cost_estimate=cost(0, 4 * values[0].size),
        name="hold",
    )(*values, *earlier)


def join_kernel(*refs):
    start = 0
    for part in refs[:-2]:
        size = part.shape[0]
        refs[-1][pl.ds(start, size), :] = part[...]
        start += size


def join(parts, earlier):
    shape = (sum(part.shape[0] for part in parts), parts[0].shape[1])
    return pl.pallas_call(
        join_kernel,
        in_specs=[VMEM] * len(parts) + [ANY],
        out_specs=VMEM,
        out_shape=jax.ShapeDtypeStruct(shape, parts[0].dtype),
        compiler_params=params(8),
        cost_estimate=cost(0, 4 * shape[0] * shape[1]),
        name="join",
    )(*parts, earlier)


def gram_steps(places, left_ref, ins, held, sems):
    slots, size = held.shape[:2]
    column = lax.axis_index("col")
    share = left_ref.shape[0] // lax.axis_size("col")
    blocks = [
        (flip, offset + start, ref, start)
        for (flip, offset), ref in zip(places, ins)
        for start in range(0, ref.shape[0], size)
    ]

    def copy(j):
        flip, offset = blocks[j][:2]
        start = pl.multiple_of((column ^ flip) * share + offset, 256)
        return pltpu.make_async_copy(left_ref.at[pl.ds(start, size)], held.at[j % slots], sems.at[j % slots])

    def begin():
        for j in range(min(slots, len(blocks))):
            copy(j).start()

    def finish(total):
        for j, (_, _, ref, start) in enumerate(blocks):
            copy(j).wait()
            product = dot0(ref[pl.ds(start, size), :], held[j % slots])
            total = product if total is None else total + product
            if j + slots < len(blocks):
                copy(j + slots).start()
        return total

    return begin, finish


def gram_kernel(places, has_total, left_ref, *refs):
    count = len(places)
    out_ref, held, sems = refs[-3:]
    begin, finish = gram_steps(places, left_ref, refs[:count], held, sems)
    begin()
    out_ref[...] = finish(refs[count][...] if has_total else None)


def gram_of(resident, pieces, places, total=None, earlier=()):
    width = pieces[0].shape[1]
    columns = resident.shape[1]
    slots, block = 4, math.gcd(2048 * 3072, *(piece.shape[0] for piece in pieces))
    height = sum(piece.shape[0] for piece in pieces)
    return pl.pallas_call(
        functools.partial(gram_kernel, places, total is not None),
        in_specs=[HBM] + [VMEM] * (len(pieces) + (total is not None)) + [ANY] * len(earlier),
        out_specs=VMEM,
        out_shape=jax.ShapeDtypeStruct((width, columns), jnp.float32),
        scratch_shapes=[
            pltpu.VMEM((slots, block, columns), jnp.bfloat16),
            pltpu.SemaphoreType.DMA((slots,)),
        ],
        compiler_params=params(16),
        cost_estimate=cost(2 * height * columns * width, 2 * height * (columns + width)),
        name="gram_of",
    )(in_hbm(resident), *pieces, *([] if total is None else [total]), *earlier)


def tiles_kernel(places, away, rows_ref, *refs):
    count = len(places)
    ins, outs, (table, taken) = refs[:count], refs[count + 1 - away : -2], refs[-2:]
    column = lax.axis_index("col")
    share = table.shape[0] // lax.axis_size("col")
    for (flip, offset), ref in zip(places, ins):
        widen(table, (column ^ flip) * share + offset, ref)
    half = taken.shape[0]
    start = list_starts(2 * half)[away] + column % 2 * half
    take_rows(lambda i: rows_ref[start + i], table, taken, 0, half)
    size = outs[0].shape[0]
    for j, out_ref in enumerate(outs):
        out_ref[...] = taken[pl.ds(j * size, size), :].astype(jnp.bfloat16)
    if away:
        row, rows = lax.axis_index("row"), lax.axis_size("row")

        @pl.when((row == 0) | (row == rows - 1))
        def _():
            for out_ref in outs:
                out_ref[...] = jnp.zeros(out_ref.shape, out_ref.dtype)


def pick_tiles(lists, pieces, places, total, away, parts, *earlier):
    width = pieces[0].shape[1]
    half = lists.shape[0] // 4
    return pl.pallas_call(
        functools.partial(tiles_kernel, places, away),
        in_specs=[SMEM] + [VMEM] * len(pieces) + [ANY] * len(earlier),
        out_specs=[VMEM] * parts,
        scratch_shapes=[pltpu.VMEM((total, width), jnp.float32), pltpu.VMEM((half, width), jnp.float32)],
        out_shape=[jax.ShapeDtypeStruct((half // parts, width), jnp.bfloat16)] * parts,
        compiler_params=params(20),
        cost_estimate=cost(0, 4 * total * width),
        name="pick_tiles",
    )(lists, *pieces, *earlier)


def finish_kernel(first_ref, second_ref, mine_ref, other_ref, total_ref, out_ref):
    half = mine_ref.shape[0] // 2
    core = lax.axis_index("col") % 2
    total = total_ref[...]
    for j, left in enumerate((first_ref, second_ref)):
        for flip, tiles in enumerate((mine_ref, other_ref)):
            rows = left[pl.ds(pl.multiple_of((core ^ flip) * half, half), half), :]
            total = total + dot0(tiles[pl.ds(j * half, half), :], rows)
    out_ref[...] = total.T


def finish(first, second, mine, other, total):
    arrays = (first, second, mine, other, total)
    return pl.pallas_call(
        finish_kernel,
        in_specs=[VMEM] * len(arrays),
        out_specs=VMEM,
        out_shape=jax.ShapeDtypeStruct(total.shape[::-1], jnp.float32),
        compiler_params=params(12),
        cost_estimate=cost(4 * first.size * mine.shape[1], 4 * first.size),
        name="finish",
    )(*arrays)


def shards(panel, stiffness, mass, resident, face_rows, counts):
    slots, nodes, width = panel.shape[1:]
    cols, rows = lax.axis_size("col"), lax.axis_size("row")
    resident = resident[0]
    columns = resident.shape[1]
    weights = mass[0].reshape(slots, 1, nodes)

    def permute(value, move):
        pairs = []
        for source in range(cols * rows):
            column, row = move(*divmod(source, rows))
            pairs.append((source, column * rows + row))
        return lax.ppermute(value, AXES, pairs)

    def across(value):
        return permute(value, lambda c, r: (c ^ 2, r))

    def sibling(value):
        return permute(value, lambda c, r: (c ^ 1, r))

    column, row = lax.axis_index("col"), lax.axis_index("row")
    share = slots * nodes
    per = slots // sum(SPLIT)
    second = per * SPLIT[0]
    offsets = (0, second * nodes)
    lists = face_rows[0].reshape(-1)
    stiffness, panel = stiffness[0], panel[0]
    pieces, far = [], []
    for first, elements in ((0, second), (second, slots - second)):
        pieces.append(apply_chunk(counts, stiffness, panel, weights, first, elements, pieces))
        far.append(across(pieces[-1]))
    first_rows, second_rows, *own = pick_resident(lists, resident, pieces, far[0])
    pieces = own + [sibling(piece) for piece in own]
    places = [(flip, offset) for flip in (0, 1) for offset in (0, share // 2)]
    places[2:2] = [(2, 0)]
    places.append((3, 0))
    total = gram_of(resident, pieces, places)
    last = [far[1], sibling(hold([far[1]], (1,), total)[0])]
    last_places = [(2, offsets[1]), (3, offsets[1])]

    rest = (lists, pieces + last, places + last_places, resident.shape[0])
    (away,) = pick_tiles(*rest, 1, 1)
    toward = pick_tiles(*rest, 0, 2, away)
    total = gram_of(resident, last, last_places, total, (toward[0],))

    def beside(c, r):
        return c, (r + 1 if r % 2 else r - 1) % rows

    met = [permute(part, lambda c, r: (c, r ^ 1)) for part in toward] + [permute(away, beside)]
    mine = join(met, total)
    gram = finish(first_rows, second_rows, mine, sibling(mine), total)

    own_rows = columns // rows
    received = lax.all_to_all(gram.reshape(rows, own_rows, width), "row", 0, 0)
    return jnp.sum(received, axis=0)


def solution(mesh):
    in_specs = (
        P("row", "col", None, None),
        P("row", "col", None, None),
        P("row", "col", None),
        P("row", None, "col"),
        P("row", None, None),
        P("row"),
    )
    out_specs = P(("col", "row"), None)
    return jax.shard_map(shards, mesh=mesh, in_specs=in_specs, out_specs=out_specs, check_vma=False)
```
